256 devices in a mesh: seq: 128 (over x, y, z_lo, core), head: 2 (over z_hi).
Axes of the slice: x: 4, y: 4, z: 8 (z_hi: 2, z_lo: 4; z = z_hi * 4 + z_lo), core: 2. Of those that a mesh axis runs over, the one named last changes fastest.
Arguments:
- queries: bfloat16 [32768, 3584], P('seq', 'head'), may hold values from -64 to 64, as said below
- keys: bfloat16 [32768, 512], P('seq', 'head'), may hold values from -4 to 4, as said below
- values: bfloat16 [32768, 512], P('seq', 'head'), may hold values from -6 to 6
- vert_blocks: int32 [4, 64], P('head'), may hold values from 0 to 511, as said below
- slash_offsets: int32 [4, 3], P('head'), may hold values from 0 to 4, as said below
Outputs:
- attended: bfloat16 [32768, 3584], P('seq', 'head')
The draws below stay inside these ranges and needn't reach their ends.
Inputs may be any that keep to these rules, and one draw needn't show every extreme that they name: `vert_blocks`: for each KV head, 64 distinct key block indices in increasing order; the range of 4 blocks of one device holds at most one of them; block 0 and the last block of the prompt are always among them. `slash_offsets`: for each KV head, 3 distinct offsets; 0 and 4 are always among them. Real-valued queries. Real-valued keys.
All inputs are finite; a program needn't handle non-finite values.
Results may differ from the reference program's by a relative error of at most 0.0049.
Values may be sent and summed in bfloat16 or wider, within the bound.
No kernel may reach another device: no remote copies, remote signals or barrier semaphores. Data moves between devices by JAX's collectives and lax.ppermute only.
A program may use at most 64 MiB of HBM per device.

```python
import jax
import jax.numpy as jnp
from jax import lax

HD = 128
KVH = 4
GROUP = 7
BLK = 64
NS = 3
TOK_DEV = 256
SEQ = 32768
NV = 64


def key_field(key):
    raw = jax.random.normal(jax.random.fold_in(key, 11), (SEQ, KVH * HD), jnp.float32)
    return jnp.clip(raw, -4.0, 4.0)


def draw_keys(key, part):
    return key_field(key).astype(jnp.bfloat16)


def draw_queries(key, part):
    raw = 2.5 * jax.random.normal(jax.random.fold_in(key, 21), (SEQ, KVH * GROUP * HD), jnp.float32)
    return jnp.clip(raw, -64.0, 64.0).astype(jnp.bfloat16)


def draw_vert_blocks(key, part):
    devices = SEQ // TOK_DEV
    per_dev = TOK_DEV // BLK
    listing = []
    for kv_head in range(KVH):
        middle = jax.random.permutation(jax.random.fold_in(key, 100 + kv_head), devices - 2)[:NV - 2] + 1
        chosen = jnp.sort(jnp.concatenate([jnp.zeros((1,), jnp.int32), middle.astype(jnp.int32), jnp.full((1,), devices - 1, jnp.int32)]))
        inside = jax.random.randint(jax.random.fold_in(key, 200 + kv_head), (NV,), 0, per_dev)
        slot_index = jnp.arange(NV)
        inside = jnp.where(slot_index == 0, 0, jnp.where(slot_index == NV - 1, per_dev - 1, inside))
        listing.append(chosen * per_dev + inside)
    return jnp.stack(listing).astype(jnp.int32)


def draw_slash_offsets(key, part):
    largest = TOK_DEV // BLK
    listing = []
    for kv_head in range(KVH):
        middle = jax.random.permutation(jax.random.fold_in(key, 300 + kv_head), largest - 1)[:NS - 2] + 1
        listing.append(jnp.concatenate([jnp.zeros((1,), jnp.int32), middle.astype(jnp.int32), jnp.full((1,), largest, jnp.int32)]))
    return jnp.stack(listing).astype(jnp.int32)


def level_of(rng, shape, split, smallest, high):
    factor_of, own = 1.0, jax.random.fold_in(rng, 6)
    for dim, blocks in split:
        draws = jnp.exp(jax.random.uniform(jax.random.fold_in(own, dim), (blocks,), jnp.float32, smallest / len(split), high / len(split)))
        factor_of = factor_of * jnp.repeat(draws, shape[dim] // blocks).reshape([-1 if axis == dim else 1 for axis in range(len(shape))])
    return factor_of


def gaussian(rng, shape, scale, reach, shards=(), held_as=jnp.bfloat16):
    loudness = level_of(rng, shape, shards, -0.22, 0.18) if shards else 1.0
    drawn = jax.random.normal(rng, shape, jnp.float32) * scale * loudness
    return jnp.minimum(jnp.maximum(drawn, -reach), reach).astype(held_as)


def setup_inputs(seed: int = 0) -> dict:
    arg_keys = jax.random.split(jax.random.key(seed), 6)
    queries = draw_queries(jax.random.fold_in(arg_keys[5], 71), 0)
    keys = draw_keys(jax.random.fold_in(arg_keys[5], 71), 0)
    values = gaussian(arg_keys[2], (SEQ, KVH * HD), 1.0, 6.0, ((0, 128), (1, 2)))
    vert_blocks = draw_vert_blocks(jax.random.fold_in(arg_keys[5], 71), 0)
    slash_offsets = draw_slash_offsets(jax.random.fold_in(arg_keys[5], 71), 0)
    return dict(queries=queries, keys=keys, values=values, vert_blocks=vert_blocks, slash_offsets=slash_offsets)


def reference(queries, keys, values, vert_blocks, slash_offsets):
    seq_len = queries.shape[0]
    block_count = seq_len // BLK
    vert_count = vert_blocks.shape[1]
    query_tiles = queries.reshape(block_count, BLK, KVH, GROUP, HD)
    key_tiles = keys.reshape(block_count, BLK, KVH, HD)
    value_tiles = values.reshape(block_count, BLK, KVH, HD)
    head_index = jnp.arange(KVH, dtype=jnp.int32)[:, None]
    inner = jnp.arange(BLK, dtype=jnp.int32)
    vert_keys = key_tiles[vert_blocks, :, head_index, :].reshape(KVH, vert_count * BLK, HD)
    vert_values = value_tiles[vert_blocks, :, head_index, :].reshape(KVH, vert_count * BLK, HD)
    vert_pos = (vert_blocks[:, :, None] * BLK + inner[None, None, :]).reshape(KVH, vert_count * BLK)
    vert_ok = jnp.ones((KVH, vert_count * BLK), dtype=bool)

    def one_block(index):
        query_pos = index * BLK + inner
        band = index - slash_offsets
        safe = jnp.maximum(band, 0).astype(jnp.int32)
        band_keys = key_tiles[safe, :, head_index, :].reshape(KVH, NS * BLK, HD)
        band_values = value_tiles[safe, :, head_index, :].reshape(KVH, NS * BLK, HD)
        band_ok = (band >= 0) & jnp.logical_not(jnp.any(band[:, :, None] == vert_blocks[:, None, :], axis=2))
        band_pos = (band[:, :, None] * BLK + inner[None, None, :]).reshape(KVH, NS * BLK)
        band_ok_keys = jnp.repeat(band_ok, BLK, axis=1)
        all_keys = jnp.concatenate([vert_keys, band_keys], axis=1).astype(jnp.float32)
        all_values = jnp.concatenate([vert_values, band_values], axis=1).astype(jnp.float32)
        all_pos = jnp.concatenate([vert_pos, band_pos], axis=1)
        all_ok = jnp.concatenate([vert_ok, band_ok_keys], axis=1)
        visible = all_ok[:, None, :] & (all_pos[:, None, :] <= query_pos[None, :, None])
        query_block = query_tiles[index].astype(jnp.float32)
        scores = jnp.einsum("thgc,hkc->hgtk", query_block, all_keys) * (HD ** -0.5)
        scores = jnp.where(visible[:, None, :, :], scores, -1e30)
        largest = jnp.max(scores, axis=3, keepdims=True)
        weights = jnp.where(visible[:, None, :, :], jnp.exp(scores - largest), 0.0)
        totals = jnp.sum(weights, axis=3)
        rounded = lax.optimization_barrier(weights.astype(jnp.bfloat16)).astype(jnp.float32)
        mixed = jnp.einsum("hgtk,hkc->hgtc", rounded, all_values) / totals[:, :, :, None]
        return jnp.transpose(mixed, (2, 0, 1, 3)).reshape(BLK, KVH * GROUP * HD).astype(jnp.bfloat16)

    blocks_out = lax.map(one_block, jnp.arange(block_count, dtype=jnp.int32))
    return blocks_out.reshape(seq_len, KVH * GROUP * HD)
```

```python
import functools

import jax
import jax.numpy as jnp
import numpy as np
from jax import lax
from jax.experimental import pallas as pl
from jax.experimental.pallas import tpu as pltpu
from jax.sharding import PartitionSpec as P

HD = 128
GROUP = 7
BLK = 64
NV = 64
ROWS = 256
HALF = 32
COLS = GROUP * HD
DIMS = (4, 4, 4, 2)
X, Y, Z, CORE = 0, 1, 2, 3
SCALE = HD ** (-0.5) * 1.4426950408889634
LIMIT = 2.0**100
CHUNK = 512
CAPACITY = 2 * NV * HALF + CHUNK
NT = (((1,), (1,)), ((), ()))
VMEM_LIMIT = 48 * 1024 * 1024

vmem = pl.BlockSpec(memory_space=pltpu.VMEM)
smem = pl.BlockSpec(memory_space=pltpu.SMEM)


def partner_route(axis, mask):
    ids = np.arange(128).reshape(DIMS)
    route = []
    for place in np.ndindex(*DIMS):
        other = list(place)
        other[axis] ^= mask
        route.append((int(ids[place]), int(ids[tuple(other)])))
    return route


def swap(block, axis, mask):
    return lax.ppermute(block, "seq", partner_route(axis, mask))


def coords():
    device = lax.axis_index("seq")
    return device, device >> 5, (device >> 3) & 3, (device >> 1) & 3, device & 1


def prep_kernel(vert_ref, keys_ref, values_ref, keep_ref, send_ref):
    device, _, _, _, core = coords()
    first = device * (ROWS // BLK)

    def find(index, found):
        out = []
        for head in range(2):
            rel = vert_ref[head, index] - first
            inside = (rel >= 0) & (rel < ROWS // BLK)
            out.append(jnp.where(inside, rel, found[head]))
        return tuple(out)

    found = lax.fori_loop(0, NV, find, (jnp.int32(0), jnp.int32(0)))
    for head in range(2):
        cols = slice(head * HD, (head + 1) * HD)
        start = pl.ds(pl.multiple_of(found[head] * BLK, BLK), BLK)

        def fill(out_ref, cols=cols, start=start):
            for which, src in enumerate((keys_ref, values_ref)):
                out_ref[which, :ROWS] = src[:, cols]
                out_ref[which, ROWS:] = src[start, cols]

        @pl.when(core == head)
        def _(fill=fill):
            fill(keep_ref)

        @pl.when(core != head)
        def _(fill=fill):
            fill(send_ref)


def prep(vert_blocks, keys, values):
    shape = jax.ShapeDtypeStruct((2, ROWS + BLK, HD), jnp.bfloat16)
    return pl.pallas_call(
        prep_kernel,
        out_shape=(shape, shape),
        in_specs=[smem, vmem, vmem],
        out_specs=(vmem, vmem),
        name="prep",
    )(vert_blocks, keys, values)


def band_kernel(
    vert_ref, slash_ref, own_ref, other_ref, keep_ref, recv_ref, prev_ref,
    acc_ref, stat_ref, key_ref, value_ref, flag_ref,
):
    device, _, _, _, core = coords()
    chip = device >> 1
    base = chip * 8 - 4
    middle = slash_ref[core, 0] + slash_ref[core, 1] + slash_ref[core, 2] - 4
    value_ref[:, HD:] = jnp.ones((3 * ROWS, HD), jnp.bfloat16)
    for src, place in ((prev_ref, 0), (keep_ref, 1 + core), (recv_ref, 2 - core)):
        rows = pl.ds(pl.multiple_of(place * ROWS, ROWS), ROWS)
        key_ref[rows, :] = src[0, :ROWS]
        value_ref[rows, :HD] = src[1, :ROWS]
    for slot in range(12):
        flag_ref[slot] = 0

    def mark(index, found):
        rel = vert_ref[core, index] - base
        inside = (rel >= 0) & (rel < 12)

        @pl.when(inside)
        def _():
            flag_ref[rel] = 1

        first = jnp.where((rel >= 4) & (rel < 8), rel, found[0])
        second = jnp.where((rel >= 8) & (rel < 12), rel, found[1])
        return first, second

    vert_first, vert_second = lax.fori_loop(0, NV, mark, (jnp.int32(99), jnp.int32(99)))
    row = lax.broadcasted_iota(jnp.int32, (BLK, 6 * BLK), 0)
    col = lax.broadcasted_iota(jnp.int32, (BLK, 6 * BLK), 1)
    piece = col // BLK
    diagonal = (piece == 0) & (col <= row)
    lane = lax.broadcasted_iota(jnp.int32, (BLK, HD), 1)
    for half, q_ref in enumerate((own_ref, other_ref)):
        chip_half = core if half == 0 else 1 - core

        def block_step(step, _, half=half, q_ref=q_ref, chip_half=chip_half):
            local = chip_half * 4 + step
            place = local + 4
            spots = [place, place - middle, place - 4, vert_first, vert_second]
            on = [None]
            for spot in spots[1:3]:
                on.append((base + spot >= 0) & (flag_ref[spot] == 0))
            for spot in spots[3:]:
                on.append(spot < place)
            allowed = diagonal
            for number in range(1, 5):
                allowed = allowed | ((piece == number) & (jnp.where(on[number], 1, 0) == 1))
            safe = [jnp.where(spot < 12, spot, 0) for spot in spots] + [place]
            windows = [pl.ds(pl.multiple_of(spot * BLK, BLK), BLK) for spot in safe]
            keys_here = jnp.concatenate([key_ref[w, :] for w in windows], axis=0)
            values_here = jnp.concatenate([value_ref[w, :] for w in windows], axis=0)
            q_rows = pl.ds(pl.multiple_of(step * BLK, BLK), BLK)
            queries = jnp.concatenate(
                [q_ref[q_rows, g * HD : (g + 1) * HD] for g in range(GROUP)], axis=0
            )
            scores = lax.dot_general(queries, keys_here, NT, preferred_element_type=jnp.float32)
            stat = jnp.zeros((BLK, HD), jnp.float32)
            weights = []
            for g in range(GROUP):
                part = jnp.where(allowed, scores[g * BLK : (g + 1) * BLK] * SCALE, -1e30)
                largest = jnp.max(part, axis=1, keepdims=True)
                weights.append(jnp.exp2(part - largest).astype(jnp.bfloat16))
                stat = jnp.where(lane == g, largest, stat)
            mixed = jnp.dot(
                jnp.concatenate(weights, axis=0), values_here, preferred_element_type=jnp.float32
            )
            for g in range(GROUP):
                part = mixed[g * BLK : (g + 1) * BLK]
                acc_ref[half, g, q_rows, :] = part[:, :HD]
                stat = jnp.where(lane == GROUP + g, part[:, HD:], stat)
            stat_ref[half, q_rows, :] = stat
            return 0

        lax.fori_loop(0, 4, block_step, 0)


STATE = (
    jax.ShapeDtypeStruct((2, GROUP, ROWS, HD), jnp.float32),
    jax.ShapeDtypeStruct((2, ROWS, HD), jnp.float32),
)


def band(vert_blocks, slash_offsets, own, other, keep, recv, prev):
    return pl.pallas_call(
        band_kernel,
        out_shape=STATE,
        in_specs=[smem, smem] + [vmem] * 5,
        out_specs=(vmem, vmem),
        scratch_shapes=[
            pltpu.VMEM((3 * ROWS, HD), jnp.bfloat16),
            pltpu.VMEM((3 * ROWS, 2 * HD), jnp.bfloat16),
            pltpu.SMEM((12,), jnp.int32),
        ],
        compiler_params=pltpu.CompilerParams(vmem_limit_bytes=VMEM_LIMIT),
        name="band",
    )(vert_blocks, slash_offsets, own, other, keep, recv, prev)


def vertical_kernel(sources, last, *refs):
    count = len(sources)
    vert_ref, own_ref, other_ref, acc_in, stat_in = refs[:5]
    pieces = refs[5 : 5 + count]
    outs = refs[5 + count : 7 + count]
    key_ref, value_ref, acc_ref, max_ref, factor_ref = refs[7 + count :]
    device, x0, y0, z0, core = coords()
    visible = (device >> 1) * 8
    value_ref[:, HD:] = jnp.ones((CAPACITY, HD), jnp.bfloat16)

    def place(index, filled):
        block = vert_ref[core, index]
        owner = block >> 2
        x, y = (owner >> 5) ^ x0, ((owner >> 3) & 3) ^ y0
        z, c = ((owner >> 1) & 3) ^ z0, owner & 1
        seen = block < visible
        for (kind, mask, low, size), src in zip(sources, pieces):
            outer, inner = (x, y) if kind == "a" else (y, x)
            here = seen & (outer == mask) & (inner >= low) & (inner < low + size)

            @pl.when(here)
            def _(src=src, inner=inner, low=low, filled=filled):
                rows = pl.ds(pl.multiple_of(filled * HALF, HALF), HALF)
                key_ref[rows, :] = src[inner - low, z, c, 0]
                value_ref[rows, :HD] = src[inner - low, z, c, 1]

            filled = filled + jnp.where(here, 1, 0)
        return filled

    filled = lax.fori_loop(0, NV, place, jnp.int32(0))
    for extra in range(CHUNK // HALF):
        rows = pl.ds(pl.multiple_of((filled + extra) * HALF, HALF), HALF)
        value_ref[rows, :HD] = jnp.zeros((HALF, HD), jnp.bfloat16)
    total = filled * HALF
    full = total // CHUNK
    rest = total - full * CHUNK
    col = lax.broadcasted_iota(jnp.int32, (ROWS, CHUNK), 1)
    lane = lax.broadcasted_iota(jnp.int32, (ROWS, HD), 1)

    for half, q_ref in enumerate((own_ref, other_ref)):
        stat = stat_in[half]
        for g in range(GROUP):
            max_ref[g] = jnp.broadcast_to(stat[:, g : g + 1], (ROWS, HD))
            factor_ref[g] = jnp.ones((ROWS, HD), jnp.float32)

        def scores_of(g, rows, masked, q_ref=q_ref):
            raw = lax.dot_general(
                q_ref[:, g * HD : (g + 1) * HD],
                key_ref[rows, :],
                NT,
                preferred_element_type=jnp.float32,
            )
            scaled = raw * SCALE
            return jnp.where(col < rest, scaled, -1e30) if masked else scaled

        def chunk_rows(step):
            return pl.ds(pl.multiple_of(step * CHUNK, CHUNK), CHUNK)

        def accumulate():
            for g in range(GROUP):
                acc_ref[g] = jnp.zeros((ROWS, 2 * HD), jnp.float32)

            def one(step, masked):
                rows = chunk_rows(step)
                for g in range(GROUP):
                    largest = max_ref[g]
                    scaled = scores_of(g, rows, masked)
                    shifted = scaled - jnp.concatenate([largest] * (CHUNK // HD), axis=1)
                    weights = jnp.exp2(shifted).astype(jnp.bfloat16)
                    acc_ref[g] += jnp.dot(
                        weights, value_ref[rows, :], preferred_element_type=jnp.float32
                    )

            def step_full(step, _):
                one(step, False)
                return 0

            lax.fori_loop(0, full, step_full, 0)

            @pl.when(rest > 0)
            def _():
                one(full, True)

        accumulate()
        largest_sum = acc_ref[0][:, HD:]
        for g in range(1, GROUP):
            largest_sum = jnp.maximum(largest_sum, acc_ref[g][:, HD:])

        @pl.when(jnp.logical_not(jnp.max(largest_sum) <= LIMIT))
        def _():
            def raise_max(step, masked):
                rows = chunk_rows(step)
                for g in range(GROUP):
                    top = jnp.max(scores_of(g, rows, masked), axis=1, keepdims=True)
                    max_ref[g] = jnp.maximum(max_ref[g], top)

            def step_full(step, _):
                raise_max(step, False)
                return 0

            lax.fori_loop(0, full, step_full, 0)

            @pl.when(rest > 0)
            def _():
                raise_max(full, True)

            for g in range(GROUP):
                factor_ref[g] = jnp.exp2(stat[:, g : g + 1] - max_ref[g])
            accumulate()

        new_stat = stat
        for g in range(GROUP):
            factor = factor_ref[g]
            acc = acc_in[half, g] * factor + acc_ref[g][:, :HD]
            sums = stat[:, GROUP + g : GROUP + g + 1] * factor + acc_ref[g][:, HD:]
            if last:
                outs[half][:, g * HD : (g + 1) * HD] = (acc / sums).astype(jnp.bfloat16)
            else:
                outs[0][half, g] = acc
                new_stat = jnp.where(lane == g, max_ref[g], new_stat)
                new_stat = jnp.where(lane == GROUP + g, sums, new_stat)
        if not last:
            outs[1][half] = new_stat


def vertical(name, vert_blocks, own, other, state, pieces, last=False):
    sources = tuple(source for source, _ in pieces)
    result = jax.ShapeDtypeStruct((ROWS, COLS), jnp.bfloat16)
    return pl.pallas_call(
        functools.partial(vertical_kernel, sources, last),
        out_shape=(result, result) if last else STATE,
        in_specs=[smem] + [vmem] * (4 + len(pieces)),
        out_specs=(vmem, vmem),
        scratch_shapes=[
            pltpu.VMEM((CAPACITY, HD), jnp.bfloat16),
            pltpu.VMEM((CAPACITY, 2 * HD), jnp.bfloat16),
            pltpu.VMEM((GROUP, ROWS, 2 * HD), jnp.float32),
            pltpu.VMEM((GROUP, ROWS, HD), jnp.float32),
            pltpu.VMEM((GROUP, ROWS, HD), jnp.float32),
        ],
        compiler_params=pltpu.CompilerParams(vmem_limit_bytes=VMEM_LIMIT),
        name=name,
    )(vert_blocks, own, other, *state, *[piece for _, piece in pieces])


def body(queries, keys, values, vert_blocks, slash_offsets):
    core = lax.axis_index("seq") & 1
    keep, send = prep(vert_blocks, keys, values)
    recv = swap(send, CORE, 1)
    own = lax.dynamic_slice(queries, (0, core * COLS), (ROWS, COLS))
    foreign = lax.dynamic_slice(queries, (0, (1 - core) * COLS), (ROWS, COLS))
    other = swap(foreign, CORE, 1)
    mine, theirs = keep[:, ROWS:], recv[:, ROWS:]
    slots = jnp.where(core == 0, jnp.stack([mine, theirs]), jnp.stack([theirs, mine]))
    one = jnp.stack([slots, swap(slots, Z, 1)])
    two = jnp.concatenate([one, swap(one, Z, 2)])
    part_a, part_b = two[:, :, :, :HALF], two[:, :, :, HALF:]
    tail = jnp.where(core == 1, keep[:, :ROWS], recv[:, :ROWS])
    prev = lax.ppermute(tail, "seq", [(i, i + 2) for i in range(126)])
    line_a, line_b = [part_a] + [None] * 3, [part_b] + [None] * 3
    for mask in (1, 3, 2):
        line_a[mask] = swap(part_a, Y, mask)
        line_b[mask] = swap(part_b, X, mask)
    plane_a, plane_b = jnp.stack(line_a), jnp.stack(line_b)
    a1, b1 = swap(plane_a, X, 1), swap(plane_b, Y, 1)
    a3, b3 = swap(plane_a, X, 3), swap(plane_b, Y, 3)
    a2_low, a2_high = swap(a3[:2], X, 1), swap(a1[2:], X, 3)
    b2_low, b2_high = swap(b3[:2], Y, 1), swap(b1[2:], Y, 3)
    state = band(vert_blocks, slash_offsets, own, other, keep, recv, prev)
    state = vertical(
        "near", vert_blocks, own, other, state,
        [(("a", 0, 0, 4), plane_a), (("b", 0, 0, 4), plane_b)],
    )
    state = vertical(
        "middle", vert_blocks, own, other, state,
        [(("a", 1, 0, 4), a1), (("b", 1, 0, 4), b1), (("a", 3, 0, 4), a3), (("b", 3, 0, 4), b3)],
    )
    result, foreign_result = vertical(
        "far", vert_blocks, own, other, state,
        [
            (("a", 2, 0, 2), a2_low),
            (("a", 2, 2, 2), a2_high),
            (("b", 2, 0, 2), b2_low),
            (("b", 2, 2, 2), b2_high),
        ],
        last=True,
    )
    arrived = swap(foreign_result, CORE, 1)
    return jnp.where(
        core == 0,
        jnp.concatenate([result, arrived], axis=1),
        jnp.concatenate([arrived, result], axis=1),
    )


def solution(mesh):
    in_specs = (
        P("seq", "head"),
        P("seq", "head"),
        P("seq", "head"),
        P("head", None),
        P("head", None),
    )
    out_specs = P("seq", "head")
    return jax.shard_map(body, mesh=mesh, in_specs=in_specs, out_specs=out_specs, check_vma=False)
```

```python
import functools

import jax
import jax.numpy as jnp
import numpy as np
from jax import lax
from jax.experimental import pallas as pl
from jax.experimental.pallas import tpu as pltpu
from jax.sharding import PartitionSpec as P

HD = 128
GROUP = 7
BLK = 64
NV = 64
ROWS = 256
HALF = 32
COLS = GROUP * HD
DIMS = (4, 4, 4, 2)
X, Y, Z, CORE = 0, 1, 2, 3
SCALE = HD ** (-0.5) * 1.4426950408889634
LIMIT = 2.0**100
CHUNK = 512
CAPACITY = 2 * NV * HALF + CHUNK
NT = (((1,), (1,)), ((), ()))
VMEM_LIMIT = 48 * 1024 * 1024

vmem = pl.BlockSpec(memory_space=pltpu.VMEM)
smem = pl.BlockSpec(memory_space=pltpu.SMEM)


def partner_route(axis, mask):
    ids = np.arange(128).reshape(DIMS)
    route = []
    for place in np.ndindex(*DIMS):
        other = list(place)
        other[axis] ^= mask
        route.append((int(ids[place]), int(ids[tuple(other)])))
    return route


def swap(block, axis, mask):
    return lax.ppermute(block, "seq", partner_route(axis, mask))


def coords():
    device = lax.axis_index("seq")
    return device, device >> 5, (device >> 3) & 3, (device >> 1) & 3, device & 1


def prep_kernel(vert_ref, keys_ref, values_ref, keep_ref, send_ref):
    device, _, _, _, core = coords()
    first = device * (ROWS // BLK)

    def find(index, found):
        out = []
        for head in range(2):
            rel = vert_ref[head, index] - first
            inside = (rel >= 0) & (rel < ROWS // BLK)
            out.append(jnp.where(inside, rel, found[head]))
        return tuple(out)

    found = lax.fori_loop(0, NV, find, (jnp.int32(0), jnp.int32(0)))
    for head in range(2):
        cols = slice(head * HD, (head + 1) * HD)
        start = pl.ds(pl.multiple_of(found[head] * BLK, BLK), BLK)

        def fill(out_ref, cols=cols, start=start):
            for which, src in enumerate((keys_ref, values_ref)):
                out_ref[which, :ROWS] = src[:, cols]
                out_ref[which, ROWS:] = src[start, cols]

        @pl.when(core == head)
        def _(fill=fill):
            fill(keep_ref)

        @pl.when(core != head)
        def _(fill=fill):
            fill(send_ref)


def prep(vert_blocks, keys, values):
    shape = jax.ShapeDtypeStruct((2, ROWS + BLK, HD), jnp.bfloat16)
    return pl.pallas_call(
        prep_kernel,
        out_shape=(shape, shape),
        in_specs=[smem, vmem, vmem],
        out_specs=(vmem, vmem),
        name="prep",
    )(vert_blocks, keys, values)


def band_kernel(
    vert_ref, slash_ref, own_ref, other_ref, keep_ref, recv_ref, prev_ref,
    acc_ref, stat_ref, plan_ref, key_ref, value_ref, flag_ref,
):
    device, x0, y0, z0, core = coords()
    chip = device >> 1
    base = chip * 8 - 4
    middle = slash_ref[core, 0] + slash_ref[core, 1] + slash_ref[core, 2] - 4
    value_ref[:, HD:] = jnp.ones((3 * ROWS, HD), jnp.bfloat16)
    for src, place in ((prev_ref, 0), (keep_ref, 1 + core), (recv_ref, 2 - core)):
        rows = pl.ds(pl.multiple_of(place * ROWS, ROWS), ROWS)
        key_ref[rows, :] = src[0, :ROWS]
        value_ref[rows, :HD] = src[1, :ROWS]
    for slot in range(12):
        flag_ref[slot] = 0
    for source in range(10):
        plan_ref[source, 0] = 0

    def mark(index, found):
        block = vert_ref[core, index]
        rel = block - base
        owner = block >> 2
        x, y = (owner >> 5) ^ x0, ((owner >> 3) & 3) ^ y0
        where_in = ((((owner >> 1) & 3) ^ z0) << 1) | (owner & 1)

        @pl.when(block < chip * 8)
        def _():
            for first, outer, inner in ((0, x, y), (1, y, x)):
                distant = 6 + 2 * first + (inner >> 1)
                nearer = jnp.where(outer == 3, 4, 2 * outer) + first
                source = jnp.where(outer == 2, distant, nearer)
                spot = jnp.where(outer == 2, inner & 1, inner)
                number = plan_ref[source, 0]
                plan_ref[source, 1 + number] = (spot << 3) | where_in
                plan_ref[source, 0] = number + 1

        inside = (rel >= 0) & (rel < 12)

        @pl.when(inside)
        def _():
            flag_ref[rel] = 1

        first = jnp.where((rel >= 4) & (rel < 8), rel, found[0])
        second = jnp.where((rel >= 8) & (rel < 12), rel, found[1])
        return first, second

    vert_first, vert_second = lax.fori_loop(0, NV, mark, (jnp.int32(99), jnp.int32(99)))
    row = lax.broadcasted_iota(jnp.int32, (BLK, 6 * BLK), 0)
    col = lax.broadcasted_iota(jnp.int32, (BLK, 6 * BLK), 1)
    piece = col // BLK
    diagonal = (piece == 0) & (col <= row)
    lane = lax.broadcasted_iota(jnp.int32, (BLK, HD), 1)
    for half, q_ref in enumerate((own_ref, other_ref)):
        chip_half = core if half == 0 else 1 - core

        def block_step(step, _, half=half, q_ref=q_ref, chip_half=chip_half):
            local = chip_half * 4 + step
            place = local + 4
            spots = [place, place - middle, place - 4, vert_first, vert_second]
            on = [None]
            for spot in spots[1:3]:
                on.append((base + spot >= 0) & (flag_ref[spot] == 0))
            for spot in spots[3:]:
                on.append(spot < place)
            allowed = diagonal
            for number in range(1, 5):
                allowed = allowed | ((piece == number) & (jnp.where(on[number], 1, 0) == 1))
            safe = [jnp.where(spot < 12, spot, 0) for spot in spots] + [place]
            windows = [pl.ds(pl.multiple_of(spot * BLK, BLK), BLK) for spot in safe]
            keys_here = jnp.concatenate([key_ref[w, :] for w in windows], axis=0)
            values_here = jnp.concatenate([value_ref[w, :] for w in windows], axis=0)
            q_rows = pl.ds(pl.multiple_of(step * BLK, BLK), BLK)
            queries = jnp.concatenate(
                [q_ref[q_rows, g * HD : (g + 1) * HD] for g in range(GROUP)], axis=0
            )
            scores = lax.dot_general(queries, keys_here, NT, preferred_element_type=jnp.float32)
            stat = jnp.zeros((BLK, HD), jnp.float32)
            weights = []
            for g in range(GROUP):
                part = jnp.where(allowed, scores[g * BLK : (g + 1) * BLK] * SCALE, -1e30)
                largest = jnp.max(part, axis=1, keepdims=True)
                weights.append(jnp.exp2(part - largest).astype(jnp.bfloat16))
                stat = jnp.where(lane == g, largest, stat)
            mixed = jnp.dot(
                jnp.concatenate(weights, axis=0), values_here, preferred_element_type=jnp.float32
            )
            for g in range(GROUP):
                part = mixed[g * BLK : (g + 1) * BLK]
                acc_ref[half, g, q_rows, :] = part[:, :HD]
                stat = jnp.where(lane == GROUP + g, part[:, HD:], stat)
            stat_ref[half, q_rows, :] = stat
            return 0

        lax.fori_loop(0, 4, block_step, 0)


STATE = (
    jax.ShapeDtypeStruct((2, GROUP, ROWS, HD), jnp.float32),
    jax.ShapeDtypeStruct((2, ROWS, HD), jnp.float32),
)


def band(vert_blocks, slash_offsets, own, other, keep, recv, prev):
    acc, stat, plan = pl.pallas_call(
        band_kernel,
        out_shape=STATE + (jax.ShapeDtypeStruct((10, 128), jnp.int32),),
        in_specs=[smem, smem] + [vmem] * 5,
        out_specs=(vmem, vmem, smem),
        scratch_shapes=[
            pltpu.VMEM((3 * ROWS, HD), jnp.bfloat16),
            pltpu.VMEM((3 * ROWS, 2 * HD), jnp.bfloat16),
            pltpu.SMEM((12,), jnp.int32),
        ],
        compiler_params=pltpu.CompilerParams(vmem_limit_bytes=VMEM_LIMIT),
        cost_estimate=cost(7),
        name="band",
    )(vert_blocks, slash_offsets, own, other, keep, recv, prev)
    return (acc, stat), plan


def vertical_kernel(rows_of, count, last, *refs):
    plan_ref = refs[0]
    queries = refs[1 : 1 + len(rows_of)]
    acc_in, stat_in = refs[1 + len(rows_of) : 3 + len(rows_of)]
    refs = refs[3 + len(rows_of) :]
    sources, pieces = count, refs[: len(count)]
    outs = refs[len(count) : -5]
    key_ref, value_ref, acc_ref, max_ref, bad_ref = refs[-5:]
    tiles = [(index, g) for index in range(len(rows_of)) for g in range(GROUP)]
    filled = jnp.int32(0)
    for source, piece in zip(sources, pieces):

        def place(step, unused, source=source, piece=piece, filled=filled):
            code = plan_ref[source, 1 + step]
            rows = pl.ds(pl.multiple_of((filled + step) * HALF, HALF), HALF)
            key_ref[rows, :] = piece[code >> 3, (code >> 1) & 3, code & 1, 0]
            value_ref[rows, :HD] = piece[code >> 3, (code >> 1) & 3, code & 1, 1]
            value_ref[rows, HD:] = jnp.ones((HALF, HD), jnp.bfloat16)
            return unused

        here = plan_ref[source, 0]
        lax.fori_loop(0, here, place, 0)
        filled = filled + here
    chunks = (filled * HALF + CHUNK - 1) // CHUNK

    def pad(step, unused):
        rows = pl.ds(pl.multiple_of(step * HALF, HALF), HALF)
        key_ref[rows, :] = key_ref[:HALF, :]
        value_ref[rows, :] = jnp.zeros((HALF, 2 * HD), jnp.bfloat16)
        return unused

    lax.fori_loop(filled, chunks * (CHUNK // HALF), pad, 0)

    def scores_of(index, cols, rows):
        raw = lax.dot_general(
            queries[index][:, cols], key_ref[rows, :], NT, preferred_element_type=jnp.float32
        )
        return raw * SCALE

    def chunk_rows(step):
        return pl.ds(pl.multiple_of(step * CHUNK, CHUNK), CHUNK)

    for tile, (index, g) in enumerate(tiles):
        stat = stat_in[rows_of[index]]
        max_ref[tile] = jnp.broadcast_to(stat[:, g : g + 1], (ROWS, HD))
    bad_ref[0] = 1

    def attempt(number, unused):
        again = bad_ref[0] == 1

        @pl.when(again & (number == 1))
        def _():
            for index in range(len(rows_of)):

                def raise_max(step, unused, index=index):
                    g = step % GROUP
                    cols = pl.ds(pl.multiple_of(g * HD, HD), HD)
                    scaled = scores_of(index, cols, chunk_rows(step // GROUP))
                    top = jnp.max(scaled, axis=1, keepdims=True)
                    max_ref[index * GROUP + g] = jnp.maximum(max_ref[index * GROUP + g], top)
                    return unused

                lax.fori_loop(0, chunks * GROUP, raise_max, 0)

        @pl.when(again)
        def _():
            for tile, (index, g) in enumerate(tiles):
                stat = stat_in[rows_of[index]]
                factor = jnp.exp2(stat[:, g : g + 1] - max_ref[tile])
                acc_ref[tile, :, :HD] = acc_in[rows_of[index], g] * factor
                acc_ref[tile, :, HD:] = stat[:, GROUP + g : GROUP + g + 1] * factor

        def accumulate(step, unused):
            rows = chunk_rows(step)
            for tile, (index, g) in enumerate(tiles):
                scaled = scores_of(index, slice(g * HD, (g + 1) * HD), rows)
                largest = jnp.concatenate([max_ref[tile]] * (CHUNK // HD), axis=1)
                weights = jnp.exp2(scaled - largest).astype(jnp.bfloat16)
                acc_ref[tile] += jnp.dot(
                    weights, value_ref[rows, :], preferred_element_type=jnp.float32
                )
            return unused

        lax.fori_loop(0, jnp.where(again, chunks, 0), accumulate, 0)
        largest_sum = acc_ref[0][:, HD:]
        for tile in range(1, len(tiles)):
            largest_sum = jnp.maximum(largest_sum, acc_ref[tile][:, HD:])
        bad_ref[0] = jnp.where(jnp.max(largest_sum) <= LIMIT, 0, 1)
        return unused

    lax.fori_loop(0, 2, attempt, 0)
    lane = lax.broadcasted_iota(jnp.int32, (ROWS, HD), 1)
    for index, half in enumerate(rows_of):
        new_stat = jnp.zeros((ROWS, HD), jnp.float32)
        for g in range(GROUP):
            tile = index * GROUP + g
            acc, sums = acc_ref[tile, :, :HD], acc_ref[tile, :, HD:]
            if last:
                outs[index][:, g * HD : (g + 1) * HD] = (acc / sums).astype(jnp.bfloat16)
            else:
                outs[0][half, g] = acc
                new_stat = jnp.where(lane == g, max_ref[tile], new_stat)
                new_stat = jnp.where(lane == GROUP + g, sums, new_stat)
        if not last:
            outs[1][half] = new_stat


def cost(micros):
    return pl.CostEstimate(flops=int(micros * 1.15e9), bytes_accessed=4 << 20, transcendentals=0)


def vertical(name, plan, queries, state, pieces, micros, rows_of=(0, 1), last=False):
    tiles = GROUP * len(rows_of)
    result = jax.ShapeDtypeStruct((ROWS, COLS), jnp.bfloat16)
    outs = (result,) * len(rows_of) if last else STATE
    return pl.pallas_call(
        functools.partial(
            vertical_kernel, rows_of, tuple(source for source, _ in pieces), last
        ),
        out_shape=outs,
        in_specs=[smem] + [vmem] * (len(rows_of) + 2 + len(pieces)),
        out_specs=(vmem,) * len(outs),
        scratch_shapes=[
            pltpu.VMEM((CAPACITY, HD), jnp.bfloat16),
            pltpu.VMEM((CAPACITY, 2 * HD), jnp.bfloat16),
            pltpu.VMEM((tiles, ROWS, 2 * HD), jnp.float32),
            pltpu.VMEM((tiles, ROWS, HD), jnp.float32),
            pltpu.SMEM((1,), jnp.int32),
        ],
        compiler_params=pltpu.CompilerParams(vmem_limit_bytes=VMEM_LIMIT),
        cost_estimate=cost(micros),
        name=name,
    )(plan, *queries, *state, *[piece for _, piece in pieces])


def body(queries, keys, values, vert_blocks, slash_offsets):
    core = lax.axis_index("seq") & 1
    keep, send = prep(vert_blocks, keys, values)
    recv = swap(send, CORE, 1)
    own = lax.dynamic_slice(queries, (0, core * COLS), (ROWS, COLS))
    foreign = lax.dynamic_slice(queries, (0, (1 - core) * COLS), (ROWS, COLS))
    other = swap(foreign, CORE, 1)
    mine, theirs = keep[:, ROWS:], recv[:, ROWS:]
    slots = jnp.where(core == 0, jnp.stack([mine, theirs]), jnp.stack([theirs, mine]))
    one = jnp.stack([slots, swap(slots, Z, 1)])
    tail = jnp.where(core == 1, keep[:, :ROWS], recv[:, :ROWS])
    prev = lax.ppermute(tail, "seq", [(i, i + 2) for i in range(126)])
    two = jnp.concatenate([one, swap(one, Z, 2)])
    part_a, part_b = two[:, :, :, :HALF], two[:, :, :, HALF:]
    state, plan = band(vert_blocks, slash_offsets, own, other, keep, recv, prev)
    line_a, line_b = [part_a] + [None] * 3, [part_b] + [None] * 3
    for mask in (1, 3, 2):
        line_a[mask] = swap(part_a, Y, mask)
        line_b[mask] = swap(part_b, X, mask)
    plane_a, plane_b = jnp.stack(line_a), jnp.stack(line_b)
    plane_a, plane_b, state, plan = lax.optimization_barrier((plane_a, plane_b, state, plan))
    a1, b1 = swap(plane_a, X, 1), swap(plane_b, Y, 1)
    a3, b3 = swap(plane_a, X, 3), swap(plane_b, Y, 3)
    q = (own, other)
    state = vertical("near", plan, q, state, [(0, plane_a), (1, plane_b)], 6)
    a1, b1, a3, b3, state = lax.optimization_barrier((a1, b1, a3, b3, state))
    a2_low, a2_high = swap(a3[:2], X, 1), swap(a1[2:], X, 3)
    b2_low, b2_high = swap(b3[:2], Y, 1), swap(b1[2:], Y, 3)
    state = vertical("middle", plan, q, state, [(2, a1), (3, b1), (4, a3), (5, b3)], 12)
    a2_low, a2_high, b2_low, b2_high, state = lax.optimization_barrier(
        (a2_low, a2_high, b2_low, b2_high, state)
    )
    far = [(6, a2_low), (7, a2_high), (8, b2_low), (9, b2_high)]
    (foreign_result,) = vertical("far", plan, q[1:], state, far, 4, (1,), True)
    arrived = swap(foreign_result, CORE, 1)
    (result,) = vertical("last", plan, q[:1], state, far, 4, (0,), True)
    return jnp.where(
        core == 0,
        jnp.concatenate([result, arrived], axis=1),
        jnp.concatenate([arrived, result], axis=1),
    )


def solution(mesh):
    in_specs = (
        P("seq", "head"),
        P("seq", "head"),
        P("seq", "head"),
        P("head", None),
        P("head", None),
    )
    out_specs = P("seq", "head")
    return jax.shard_map(body, mesh=mesh, in_specs=in_specs, out_specs=out_specs, check_vma=False)
```

```python
import functools

import jax
import jax.numpy as jnp
import numpy as np
from jax import lax
from jax.experimental import pallas as pl
from jax.experimental.pallas import tpu as pltpu
from jax.sharding import PartitionSpec as P

HD = 128
GROUP = 7
BLK = 64
NV = 64
ROWS = 256
HALF = 32
COLS = GROUP * HD
DIMS = (4, 4, 4, 2)
X, Y, Z, CORE = 0, 1, 2, 3
SCALE = HD ** (-0.5) * 1.4426950408889634
LIMIT = 2.0**100
CHUNK = 256
UNROLL = 4
CAPACITY = 2 * NV * HALF + 2 * CHUNK
NT = (((1,), (1,)), ((), ()))
VMEM_LIMIT = 32 * 1024 * 1024

vmem = pl.BlockSpec(memory_space=pltpu.VMEM)
smem = pl.BlockSpec(memory_space=pltpu.SMEM)


def partner_route(axis, mask):
    ids = np.arange(128).reshape(DIMS)
    route = []
    for place in np.ndindex(*DIMS):
        other = list(place)
        other[axis] ^= mask
        route.append((int(ids[place]), int(ids[tuple(other)])))
    return route


def swap(block, axis, mask):
    return lax.ppermute(block, "seq", partner_route(axis, mask))


def cross(block):
    route = [(source, target ^ 1) for source, target in partner_route(Z, 1)]
    return lax.ppermute(block, "seq", route)


def coords():
    device = lax.axis_index("seq")
    return device, device >> 5, (device >> 3) & 3, (device >> 1) & 3, device & 1


def prep_kernel(vert_ref, keys_ref, values_ref, keep_ref, send_ref):
    device, _, _, _, core = coords()
    first = device * (ROWS // BLK)

    def find(index, found):
        out = []
        for head in range(2):
            rel = vert_ref[head, index] - first
            inside = (rel >= 0) & (rel < ROWS // BLK)
            out.append(jnp.where(inside, rel, found[head]))
        return tuple(out)

    found = lax.fori_loop(0, NV, find, (jnp.int32(0), jnp.int32(0)))
    for head in range(2):
        cols = slice(head * HD, (head + 1) * HD)
        start = pl.ds(pl.multiple_of(found[head] * BLK, BLK), BLK)

        def fill(out_ref, cols=cols, start=start):
            for which, src in enumerate((keys_ref, values_ref)):
                out_ref[which, :ROWS] = src[:, cols]
                out_ref[which, ROWS:] = src[start, cols]

        @pl.when(core == head)
        def _(fill=fill):
            fill(keep_ref)

        @pl.when(core != head)
        def _(fill=fill):
            fill(send_ref)


def prep(vert_blocks, keys, values):
    shape = jax.ShapeDtypeStruct((2, ROWS + BLK, HD), jnp.bfloat16)
    return pl.pallas_call(
        prep_kernel,
        out_shape=(shape, shape),
        in_specs=[smem, vmem, vmem],
        out_specs=(vmem, vmem),
        name="prep",
    )(vert_blocks, keys, values)


def cost(micros):
    return pl.CostEstimate(flops=int(micros * 1.15e9), bytes_accessed=4 << 20, transcendentals=0)


def plan_kernel(vert_ref, after_ref, plan_ref):
    device, x0, y0, z0, core = coords()
    chip = device >> 1
    base = chip * 8 - 4
    for source in range(8):
        plan_ref[source, 0] = 0
    for slot in range(12):
        plan_ref[8, slot] = 0
    plan_ref[8, 12] = 99
    plan_ref[8, 13] = 99

    def mark(index, unused):
        block = vert_ref[core, index]
        rel = block - base
        owner = block >> 2
        x, y = (owner >> 5) ^ x0, ((owner >> 3) & 3) ^ y0
        x, y = x ^ (x >> 1), y ^ (y >> 1)
        where_in = ((((owner >> 1) & 3) ^ z0) << 1) | (owner & 1)

        @pl.when(block < chip * 8)
        def _():
            for first, outer, inner in ((0, x, y), (1, y, x)):
                source = 2 * outer + first
                number = plan_ref[source, 0]
                plan_ref[source, 1 + number] = (inner << 3) | where_in
                plan_ref[source, 0] = number + 1

        @pl.when((rel >= 0) & (rel < 12))
        def _():
            plan_ref[8, rel] = 1

            @pl.when(rel >= 4)
            def _():
                plan_ref[8, 11 + (rel >> 2)] = rel

        return unused

    lax.fori_loop(0, NV, mark, 0)


def split_kernel(q_ref, after_ref, own_ref, foreign_ref):
    core = coords()[-1]

    @pl.when(core == 0)
    def _():
        own_ref[...] = q_ref[:, :COLS]
        foreign_ref[...] = q_ref[:, COLS:]

    @pl.when(core == 1)
    def _():
        own_ref[...] = q_ref[:, COLS:]
        foreign_ref[...] = q_ref[:, :COLS]


def split(queries, after):
    shape = jax.ShapeDtypeStruct((ROWS, COLS), jnp.bfloat16)
    return pl.pallas_call(
        split_kernel,
        out_shape=(shape, shape),
        in_specs=[vmem, pl.BlockSpec(memory_space=pl.ANY)],
        out_specs=(vmem, vmem),
        cost_estimate=cost(1.5),
        name="split",
    )(queries, after)


def make_plan(vert_blocks, after):
    return pl.pallas_call(
        plan_kernel,
        out_shape=jax.ShapeDtypeStruct((9, 128), jnp.int32),
        in_specs=[smem, pl.BlockSpec(memory_space=pl.ANY)],
        out_specs=smem,
        cost_estimate=cost(3),
        name="plan",
    )(vert_blocks, after)


def band_kernel(
    foreign, plan_ref, slash_ref, q_ref, keep_ref, recv_ref, prev_ref,
    acc_ref, max_ref, key_ref, value_ref,
):
    device, _, _, _, core = coords()
    base = (device >> 1) * 8 - 4
    middle = slash_ref[core, 0] + slash_ref[core, 1] + slash_ref[core, 2] - 4
    value_ref[:, HD:] = jnp.ones((3 * ROWS, HD), jnp.bfloat16)
    for src, place in ((prev_ref, 0), (keep_ref, 1 + core), (recv_ref, 2 - core)):
        rows = pl.ds(pl.multiple_of(place * ROWS, ROWS), ROWS)
        key_ref[rows, :] = src[0, :ROWS]
        value_ref[rows, :HD] = src[1, :ROWS]
    vert_first, vert_second = plan_ref[8, 12], plan_ref[8, 13]
    row = lax.broadcasted_iota(jnp.int32, (BLK, 6 * BLK), 0)
    col = lax.broadcasted_iota(jnp.int32, (BLK, 6 * BLK), 1)
    piece = col // BLK
    diagonal = (piece == 0) & (col <= row)
    chip_half = 1 - core if foreign else core
    for step in range(4):
        place = chip_half * 4 + (step + 4)
        spots = [place, place - middle, place - 4, vert_first, vert_second]
        on = [None]
        for spot in spots[1:3]:
            on.append((base + spot >= 0) & (plan_ref[8, spot] == 0))
        for spot in spots[3:]:
            on.append(spot < place)
        allowed = diagonal
        for number in range(1, 5):
            allowed = allowed | ((piece == number) & (jnp.where(on[number], 1, 0) == 1))
        safe = [jnp.where(spot < 12, spot, 0) for spot in spots] + [place]
        windows = [pl.ds(pl.multiple_of(spot * BLK, BLK), BLK) for spot in safe]
        keys_here = jnp.concatenate([key_ref[w, :] for w in windows], axis=0)
        values_here = jnp.concatenate([value_ref[w, :] for w in windows], axis=0)
        q_rows = slice(step * BLK, (step + 1) * BLK)
        queries = jnp.concatenate(
            [q_ref[q_rows, g * HD : (g + 1) * HD] for g in range(GROUP)], axis=0
        )
        scores = lax.dot_general(queries, keys_here, NT, preferred_element_type=jnp.float32)
        weights = []
        for g in range(GROUP):
            part = jnp.where(allowed, scores[g * BLK : (g + 1) * BLK] * SCALE, -1e30)
            largest = jnp.max(part, axis=1, keepdims=True)
            weights.append(jnp.exp2(part - largest).astype(jnp.bfloat16))
            max_ref[g, q_rows, :] = jnp.broadcast_to(largest, (BLK, HD))
        mixed = jnp.dot(
            jnp.concatenate(weights, axis=0), values_here, preferred_element_type=jnp.float32
        )
        for g in range(GROUP):
            acc_ref[g, q_rows, :] = mixed[g * BLK : (g + 1) * BLK]


STATE = (
    jax.ShapeDtypeStruct((GROUP, ROWS, 2 * HD), jnp.float32),
    jax.ShapeDtypeStruct((GROUP, ROWS, HD), jnp.float32),
)


def band(name, foreign, plan, slash_offsets, queries, keep, recv, prev):
    return pl.pallas_call(
        functools.partial(band_kernel, foreign),
        out_shape=STATE,
        in_specs=[smem, smem] + [vmem] * 4,
        out_specs=(vmem, vmem),
        scratch_shapes=[
            pltpu.VMEM((3 * ROWS, HD), jnp.bfloat16),
            pltpu.VMEM((3 * ROWS, 2 * HD), jnp.bfloat16),
        ],
        compiler_params=pltpu.CompilerParams(vmem_limit_bytes=VMEM_LIMIT),
        cost_estimate=cost(3),
        name=name,
    )(plan, slash_offsets, queries, keep, recv, prev)


def vertical_kernel(groups, begin, end, last, *refs):
    plan_ref, refs = refs[0], refs[1:]
    queries, refs = refs[:groups], refs[groups:]
    state, refs = refs[: 2 * groups], refs[2 * groups :]
    pieces, outs, scratch = refs[:end], refs[end:-5], refs[-5:]
    key_ref, value_ref, max_ref, score_ref, bad_ref = scratch
    if last:
        result_ref, acc_ref = outs
        accs = [acc_ref]
    else:
        accs = outs[::2]
    tiles = [(index, g) for index in range(groups) for g in range(GROUP)]
    ahead = 2 if len(tiles) % 2 == 0 else len(tiles)
    per_chunk = CHUNK // HALF
    counts = [plan_ref[source, 0] for source in range(end)]
    start = sum(counts[:begin], jnp.int32(0)) // per_chunk * per_chunk
    total = sum(counts, jnp.int32(0))
    stop = total if last else total // per_chunk * per_chunk
    before = jnp.int32(0)
    for source in range(end):

        low = jnp.clip(start - before, 0, counts[source])
        high = jnp.clip(stop - before, 0, counts[source])

        def place(step, unused, source=source, before=before, low=low, high=high):
            for extra in range(UNROLL):
                entry = jnp.minimum(low + step * UNROLL + extra, high - 1)
                code = plan_ref[source, 1 + entry]
                rows = pl.ds(pl.multiple_of((before + entry - start) * HALF, HALF), HALF)
                key_ref[rows, :] = pieces[source][code, 0]
                value_ref[rows, :HD] = pieces[source][code, 1]
                value_ref[rows, HD:] = jnp.ones((HALF, HD), jnp.bfloat16)
            return unused

        lax.fori_loop(0, (high - low + UNROLL - 1) // UNROLL, place, 0)
        before = before + counts[source]
    filled = stop - start
    chunks = (filled + per_chunk - 1) // per_chunk
    if last:

        def pad(step, unused):
            rows = pl.ds(pl.multiple_of(step * HALF, HALF), HALF)
            key_ref[rows, :] = key_ref[:HALF, :]
            value_ref[rows, :] = jnp.zeros((HALF, 2 * HD), jnp.bfloat16)
            return unused

        lax.fori_loop(filled, chunks * per_chunk, pad, 0)

    def scores_of(index, cols, step):
        rows = pl.ds(pl.multiple_of(step * CHUNK, CHUNK), CHUNK)
        return lax.dot_general(
            queries[index][:, cols], key_ref[rows, :], NT, preferred_element_type=jnp.float32
        )

    def tile_scores(tile, step):
        index, g = tiles[tile]
        return scores_of(index, slice(g * HD, (g + 1) * HD), step)

    for tile, (index, g) in enumerate(tiles):
        max_ref[tile] = state[2 * index + 1][g]
    bad_ref[0] = 1

    def attempt(number, unused):
        again = bad_ref[0] == 1

        @pl.when(again & (number == 0))
        def _():
            for index, g in tiles:
                accs[index][g] = state[2 * index][g]

        @pl.when(again & (number == 1))
        def _():
            for index in range(groups):

                def raise_max(step, unused, index=index):
                    g = step % GROUP
                    cols = pl.ds(pl.multiple_of(g * HD, HD), HD)
                    scaled = scores_of(index, cols, step // GROUP) * SCALE
                    top = jnp.max(scaled, axis=1, keepdims=True)
                    max_ref[index * GROUP + g] = jnp.maximum(max_ref[index * GROUP + g], top)
                    return unused

                def rescale(g, unused, index=index):
                    factor = jnp.exp2(state[2 * index + 1][g] - max_ref[index * GROUP + g])
                    accs[index][g] = state[2 * index][g] * jnp.concatenate([factor] * 2, axis=1)
                    return unused

                lax.fori_loop(0, chunks * GROUP, raise_max, 0)
                lax.fori_loop(0, GROUP, rescale, 0)

        @pl.when(again)
        def _():
            for tile in range(ahead):
                score_ref[tile] = tile_scores(tile, 0)

            def accumulate(step, unused):
                rows = pl.ds(pl.multiple_of(step * CHUNK, CHUNK), CHUNK)
                for tile, (index, g) in enumerate(tiles):
                    later = tile + ahead
                    coming = tile_scores(later % len(tiles), step + later // len(tiles))
                    largest = jnp.concatenate([max_ref[tile]] * (CHUNK // HD), axis=1)
                    shifted = score_ref[tile % ahead] * SCALE - largest
                    score_ref[tile % ahead] = coming
                    weights = jnp.exp2(shifted).astype(jnp.bfloat16)
                    accs[index][g] += jnp.dot(
                        weights, value_ref[rows, :], preferred_element_type=jnp.float32
                    )
                return unused

            lax.fori_loop(0, chunks, accumulate, 0)
            largest_sum = accs[0][0][:, HD:]
            for index, g in tiles[1:]:
                largest_sum = jnp.maximum(largest_sum, accs[index][g][:, HD:])
            bad_ref[0] = jnp.where(jnp.max(largest_sum) <= LIMIT, 0, 1)

        return unused

    lax.fori_loop(0, 2, attempt, 0)
    for tile, (index, g) in enumerate(tiles):
        if last:
            part = accs[0][g]
            result_ref[:, g * HD : (g + 1) * HD] = (part[:, :HD] / part[:, HD:]).astype(
                jnp.bfloat16
            )
        else:
            outs[2 * index + 1][g] = max_ref[tile]


def vertical(name, plan, parts, begin, pieces, micros, last=False):
    groups = len(parts)
    outs = STATE * groups
    scratch = []
    if last:
        outs = (jax.ShapeDtypeStruct((ROWS, COLS), jnp.bfloat16),)
        scratch = [pltpu.VMEM((GROUP, ROWS, 2 * HD), jnp.float32)]
    return pl.pallas_call(
        functools.partial(vertical_kernel, groups, begin, len(pieces), last),
        out_shape=outs,
        in_specs=[smem] + [vmem] * (3 * groups + len(pieces)),
        out_specs=(vmem,) * len(outs),
        scratch_shapes=scratch
        + [
            pltpu.VMEM((CAPACITY, HD), jnp.bfloat16),
            pltpu.VMEM((CAPACITY, 2 * HD), jnp.bfloat16),
            pltpu.VMEM((groups * GROUP, ROWS, HD), jnp.float32),
            pltpu.VMEM((2 if groups == 2 else GROUP, ROWS, CHUNK), jnp.float32),
            pltpu.SMEM((1,), jnp.int32),
        ],
        compiler_params=pltpu.CompilerParams(vmem_limit_bytes=VMEM_LIMIT),
        cost_estimate=cost(micros),
        name=name,
    )(plan, *[q for q, _ in parts], *[x for _, state in parts for x in state],
      *[piece.reshape(32, 2, HALF, HD) for piece in pieces])


def body(queries, keys, values, vert_blocks, slash_offsets):
    core = lax.axis_index("seq") & 1
    keep, send = prep(vert_blocks, keys, values)
    recv = swap(send, CORE, 1)
    keep_z = swap(keep[:, ROWS:], Z, 1)
    recv_z = cross(send[:, ROWS:])
    mine, theirs = jnp.stack([keep[:, ROWS:], keep_z]), jnp.stack([recv[:, ROWS:], recv_z])
    one = jnp.where(
        core == 0, jnp.stack([mine, theirs], axis=1), jnp.stack([theirs, mine], axis=1)
    )
    one_z = swap(one, Z, 2)
    plan = make_plan(vert_blocks, one)
    tail = jnp.where(core == 1, keep[:, :ROWS], recv[:, :ROWS])
    tail = tail + one_z[0, 0, :, :1, :1] * 0
    prev = lax.ppermute(tail, "seq", [(i, i + 2) for i in range(126)])
    own, foreign = split(queries, one)
    other = swap(foreign, CORE, 1)
    near_own = band("band_own", False, plan, slash_offsets, own, keep, recv, prev)
    near_other = band("band_other", True, plan, slash_offsets, other, keep, recv, prev)
    two = jnp.concatenate([one, one_z])
    near = []
    for part, axis in ((two[:, :, :, :HALF], Y), (two[:, :, :, HALF:], X)):
        line = jnp.stack([part, swap(part, axis, 1)])
        near.append(jnp.concatenate([line, swap(line, axis, 3)]))
    via_1 = [swap(piece, axis, 1) for piece, axis in zip(near, (X, Y))]
    via_3 = [swap(piece, axis, 3) for piece, axis in zip(near, (X, Y))]
    far = [swap(piece, axis, 1) for piece, axis in zip(via_3, (X, Y))]
    parts = ((own, near_own), (other, near_other))
    state = vertical("near", plan, parts, 0, near, 6)
    parts = ((own, state[:2]), (other, state[2:]))
    pieces = near + via_1 + via_3
    state = vertical("middle", plan, parts, 2, pieces, 12)
    pieces = pieces + far
    (foreign_result,) = vertical("far", plan, ((other, state[2:]),), 6, pieces, 4, True)
    arrived = swap(foreign_result, CORE, 1)
    (result,) = vertical("last", plan, ((own, state[:2]),), 6, pieces, 4, True)
    return jnp.where(
        core == 0,
        jnp.concatenate([result, arrived], axis=1),
        jnp.concatenate([arrived, result], axis=1),
    )


def solution(mesh):
    in_specs = (
        P("seq", "head"),
        P("seq", "head"),
        P("seq", "head"),
        P("head", None),
        P("head", None),
    )
    out_specs = P("seq", "head")
    return jax.shard_map(body, mesh=mesh, in_specs=in_specs, out_specs=out_specs, check_vma=False)
```

```python
import functools

import jax
import jax.numpy as jnp
import numpy as np
from jax import lax
from jax.experimental import pallas as pl
from jax.experimental.pallas import tpu as pltpu
from jax.sharding import PartitionSpec as P

HD = 128
GROUP = 7
BLK = 64
NV = 64
ROWS = 256
HALF = 32
COLS = GROUP * HD
DIMS = (4, 4, 4, 2)
X, Y, Z, CORE = 0, 1, 2, 3
SCALE = HD ** (-0.5) * 1.4426950408889634
LIMIT = 2.0**100
CHUNK = 256
UNROLL = 4
CAPACITY = 2 * NV * HALF + 2 * CHUNK
NT = (((1,), (1,)), ((), ()))
VMEM_LIMIT = 32 * 1024 * 1024

vmem = pl.BlockSpec(memory_space=pltpu.VMEM)
smem = pl.BlockSpec(memory_space=pltpu.SMEM)


def partner_route(axis, mask):
    ids = np.arange(128).reshape(DIMS)
    route = []
    for place in np.ndindex(*DIMS):
        other = list(place)
        other[axis] ^= mask
        route.append((int(ids[place]), int(ids[tuple(other)])))
    return route


def swap(block, axis, mask):
    return lax.ppermute(block, "seq", partner_route(axis, mask))


def cross(block):
    route = [(source, target ^ 1) for source, target in partner_route(Z, 1)]
    return lax.ppermute(block, "seq", route)


def coords():
    device = lax.axis_index("seq")
    return device, device >> 5, (device >> 3) & 3, (device >> 1) & 3, device & 1


def prep_kernel(
    vert_ref, keys_ref, values_ref, keep_ref, send_ref, keep_slot_ref, send_slot_ref
):
    device, _, _, _, core = coords()
    first = device * (ROWS // BLK)

    def find(index, found):
        out = []
        for head in range(2):
            rel = vert_ref[head, index] - first
            inside = (rel >= 0) & (rel < ROWS // BLK)
            out.append(jnp.where(inside, rel, found[head]))
        return tuple(out)

    found = lax.fori_loop(0, NV, find, (jnp.int32(0), jnp.int32(0)), unroll=16)
    for head in range(2):
        cols = slice(head * HD, (head + 1) * HD)
        start = pl.ds(pl.multiple_of(found[head] * BLK, BLK), BLK)

        def fill(out_ref, slot_ref, cols=cols, start=start):
            for which, src in enumerate((keys_ref, values_ref)):
                slot = src[start, cols]
                out_ref[which, :ROWS] = src[:, cols]
                out_ref[which, ROWS:] = slot
                slot_ref[which] = slot

        @pl.when(core == head)
        def _(fill=fill):
            fill(keep_ref, keep_slot_ref)

        @pl.when(core != head)
        def _(fill=fill):
            fill(send_ref, send_slot_ref)


def prep(vert_blocks, keys, values):
    shape = jax.ShapeDtypeStruct((2, ROWS + BLK, HD), jnp.bfloat16)
    slot = jax.ShapeDtypeStruct((2, BLK, HD), jnp.bfloat16)
    return pl.pallas_call(
        prep_kernel,
        out_shape=(shape, shape, slot, slot),
        in_specs=[smem, vmem, vmem],
        out_specs=(vmem, vmem, vmem, vmem),
        name="prep",
    )(vert_blocks, keys, values)


def cost(micros):
    return pl.CostEstimate(flops=int(micros * 1.15e9), bytes_accessed=4 << 20, transcendentals=0)


def plan_kernel(vert_ref, after_ref, plan_ref):
    device, x0, y0, z0, core = coords()
    chip = device >> 1
    base = chip * 8 - 4
    for source in range(8):
        plan_ref[source, 0] = 0
    for slot in range(12):
        plan_ref[8, slot] = 0
    plan_ref[8, 12] = 99
    plan_ref[8, 13] = 99

    def mark(index, unused):
        block = vert_ref[core, index]
        rel = block - base
        owner = block >> 2
        x, y = (owner >> 5) ^ x0, ((owner >> 3) & 3) ^ y0
        x, y = x ^ (x >> 1), y ^ (y >> 1)
        where_in = ((((owner >> 1) & 3) ^ z0) << 1) | (owner & 1)

        @pl.when(block < chip * 8)
        def _():
            for first, outer, inner in ((0, x, y), (1, y, x)):
                source = 2 * outer + first
                number = plan_ref[source, 0]
                plan_ref[source, 1 + number] = (inner << 3) | where_in
                plan_ref[source, 0] = number + 1

        @pl.when((rel >= 0) & (rel < 12))
        def _():
            plan_ref[8, rel] = 1

            @pl.when(rel >= 4)
            def _():
                plan_ref[8, 11 + (rel >> 2)] = rel

        return unused

    lax.fori_loop(0, NV, mark, 0)


def split_kernel(q_ref, after_ref, own_ref, foreign_ref):
    core = coords()[-1]

    @pl.when(core == 0)
    def _():
        own_ref[...] = q_ref[:, :COLS]
        foreign_ref[...] = q_ref[:, COLS:]

    @pl.when(core == 1)
    def _():
        own_ref[...] = q_ref[:, COLS:]
        foreign_ref[...] = q_ref[:, :COLS]


def split(queries, after):
    shape = jax.ShapeDtypeStruct((ROWS, COLS), jnp.bfloat16)
    return pl.pallas_call(
        split_kernel,
        out_shape=(shape, shape),
        in_specs=[vmem, vmem],
        out_specs=(vmem, vmem),
        cost_estimate=cost(1.5),
        name="split",
    )(queries, after)


def make_plan(vert_blocks, after):
    return pl.pallas_call(
        plan_kernel,
        out_shape=jax.ShapeDtypeStruct((9, 128), jnp.int32),
        in_specs=[smem, vmem],
        out_specs=smem,
        cost_estimate=cost(3),
        name="plan",
    )(vert_blocks, after)


def band_kernel(
    foreign, plan_ref, slash_ref, q_ref, keep_ref, recv_ref, prev_ref,
    acc_ref, max_ref, key_ref, value_ref,
):
    device, _, _, _, core = coords()
    base = (device >> 1) * 8 - 4
    middle = slash_ref[core, 0] + slash_ref[core, 1] + slash_ref[core, 2] - 4
    value_ref[:, HD:] = jnp.ones((3 * ROWS, HD), jnp.bfloat16)
    for src, place in ((prev_ref, 0), (keep_ref, 1 + core), (recv_ref, 2 - core)):
        rows = pl.ds(pl.multiple_of(place * ROWS, ROWS), ROWS)
        key_ref[rows, :] = src[0, :ROWS]
        value_ref[rows, :HD] = src[1, :ROWS]
    vert_first, vert_second = plan_ref[8, 12], plan_ref[8, 13]
    row = lax.broadcasted_iota(jnp.int32, (BLK, 6 * BLK), 0)
    col = lax.broadcasted_iota(jnp.int32, (BLK, 6 * BLK), 1)
    piece = col // BLK
    diagonal = (piece == 0) & (col <= row)
    chip_half = 1 - core if foreign else core
    for step in range(4):
        place = chip_half * 4 + (step + 4)
        spots = [place, place - middle, place - 4, vert_first, vert_second]
        on = [None]
        for spot in spots[1:3]:
            on.append((base + spot >= 0) & (plan_ref[8, spot] == 0))
        for spot in spots[3:]:
            on.append(spot < place)
        allowed = diagonal
        for number in range(1, 5):
            allowed = allowed | ((piece == number) & (jnp.where(on[number], 1, 0) == 1))
        safe = [jnp.where(spot < 12, spot, 0) for spot in spots] + [place]
        windows = [pl.ds(pl.multiple_of(spot * BLK, BLK), BLK) for spot in safe]
        keys_here = jnp.concatenate([key_ref[w, :] for w in windows], axis=0)
        values_here = jnp.concatenate([value_ref[w, :] for w in windows], axis=0)
        q_rows = slice(step * BLK, (step + 1) * BLK)
        queries = jnp.concatenate(
            [q_ref[q_rows, g * HD : (g + 1) * HD] for g in range(GROUP)], axis=0
        )
        scores = lax.dot_general(queries, keys_here, NT, preferred_element_type=jnp.float32)
        weights = []
        for g in range(GROUP):
            part = jnp.where(allowed, scores[g * BLK : (g + 1) * BLK] * SCALE, -1e30)
            largest = jnp.max(part, axis=1, keepdims=True)
            weights.append(jnp.exp2(part - largest).astype(jnp.bfloat16))
            max_ref[g, q_rows, :] = jnp.broadcast_to(largest, (BLK, HD))
        mixed = jnp.dot(
            jnp.concatenate(weights, axis=0), values_here, preferred_element_type=jnp.float32
        )
        for g in range(GROUP):
            acc_ref[g, q_rows, :] = mixed[g * BLK : (g + 1) * BLK]


STATE = (
    jax.ShapeDtypeStruct((GROUP, ROWS, 2 * HD), jnp.float32),
    jax.ShapeDtypeStruct((GROUP, ROWS, HD), jnp.float32),
)


def band(name, foreign, plan, slash_offsets, queries, keep, recv, prev):
    return pl.pallas_call(
        functools.partial(band_kernel, foreign),
        out_shape=STATE,
        in_specs=[smem, smem] + [vmem] * 4,
        out_specs=(vmem, vmem),
        scratch_shapes=[
            pltpu.VMEM((3 * ROWS, HD), jnp.bfloat16),
            pltpu.VMEM((3 * ROWS, 2 * HD), jnp.bfloat16),
        ],
        compiler_params=pltpu.CompilerParams(vmem_limit_bytes=VMEM_LIMIT),
        cost_estimate=cost(3),
        name=name,
    )(plan, slash_offsets, queries, keep, recv, prev)


def vertical_kernel(groups, begin, end, last, *refs):
    plan_ref, refs = refs[0], refs[1:]
    queries, refs = refs[:groups], refs[groups:]
    state, refs = refs[: 2 * groups], refs[2 * groups :]
    pieces, outs, scratch = refs[:end], refs[end:-5], refs[-5:]
    key_ref, value_ref, max_ref, score_ref, bad_ref = scratch
    if last:
        result_ref, acc_ref = outs
        accs = [acc_ref]
    else:
        accs = outs[::2]
    tiles = [(index, g) for index in range(groups) for g in range(GROUP)]
    ahead = 2 if len(tiles) % 2 == 0 else len(tiles)
    per_chunk = CHUNK // HALF
    counts = [plan_ref[source, 0] for source in range(end)]
    start = sum(counts[:begin], jnp.int32(0)) // per_chunk * per_chunk
    total = sum(counts, jnp.int32(0))
    stop = total if last else total // per_chunk * per_chunk
    before = jnp.int32(0)
    for source in range(end):

        low = jnp.clip(start - before, 0, counts[source])
        high = jnp.clip(stop - before, 0, counts[source])

        def place(step, unused, source=source, before=before, low=low, high=high):
            for extra in range(UNROLL):
                entry = jnp.minimum(low + step * UNROLL + extra, high - 1)
                code = plan_ref[source, 1 + entry]
                rows = pl.ds(pl.multiple_of((before + entry - start) * HALF, HALF), HALF)
                key_ref[rows, :] = pieces[source][code, 0]
                value_ref[rows, :HD] = pieces[source][code, 1]
                value_ref[rows, HD:] = jnp.ones((HALF, HD), jnp.bfloat16)
            return unused

        lax.fori_loop(0, (high - low + UNROLL - 1) // UNROLL, place, 0)
        before = before + counts[source]
    filled = stop - start
    chunks = (filled + per_chunk - 1) // per_chunk
    if last:

        def pad(step, unused):
            rows = pl.ds(pl.multiple_of(step * HALF, HALF), HALF)
            key_ref[rows, :] = key_ref[:HALF, :]
            value_ref[rows, :] = jnp.zeros((HALF, 2 * HD), jnp.bfloat16)
            return unused

        lax.fori_loop(filled, chunks * per_chunk, pad, 0)

    def scores_of(index, cols, step):
        rows = pl.ds(pl.multiple_of(step * CHUNK, CHUNK), CHUNK)
        return lax.dot_general(
            queries[index][:, cols], key_ref[rows, :], NT, preferred_element_type=jnp.float32
        )

    def tile_scores(tile, step):
        index, g = tiles[tile]
        return scores_of(index, slice(g * HD, (g + 1) * HD), step)

    for tile, (index, g) in enumerate(tiles):
        max_ref[tile] = state[2 * index + 1][g]
    bad_ref[0] = 1

    def attempt(number, unused):
        again = bad_ref[0] == 1

        @pl.when(again & (number == 0))
        def _():
            for index, g in tiles:
                accs[index][g] = state[2 * index][g]

        @pl.when(again & (number == 1))
        def _():
            for index in range(groups):

                def raise_max(step, unused, index=index):
                    g = step % GROUP
                    cols = pl.ds(pl.multiple_of(g * HD, HD), HD)
                    scaled = scores_of(index, cols, step // GROUP) * SCALE
                    top = jnp.max(scaled, axis=1, keepdims=True)
                    max_ref[index * GROUP + g] = jnp.maximum(max_ref[index * GROUP + g], top)
                    return unused

                def rescale(g, unused, index=index):
                    factor = jnp.exp2(state[2 * index + 1][g] - max_ref[index * GROUP + g])
                    accs[index][g] = state[2 * index][g] * jnp.concatenate([factor] * 2, axis=1)
                    return unused

                lax.fori_loop(0, chunks * GROUP, raise_max, 0)
                lax.fori_loop(0, GROUP, rescale, 0)

        @pl.when(again)
        def _():
            for tile in range(ahead):
                score_ref[tile] = tile_scores(tile, 0)

            def accumulate(step, unused):
                rows = pl.ds(pl.multiple_of(step * CHUNK, CHUNK), CHUNK)
                for tile, (index, g) in enumerate(tiles):
                    later = tile + ahead
                    coming = tile_scores(later % len(tiles), step + later // len(tiles))
                    largest = jnp.concatenate([max_ref[tile]] * (CHUNK // HD), axis=1)
                    shifted = score_ref[tile % ahead] * SCALE - largest
                    score_ref[tile % ahead] = coming
                    weights = jnp.exp2(shifted).astype(jnp.bfloat16)
                    accs[index][g] += jnp.dot(
                        weights, value_ref[rows, :], preferred_element_type=jnp.float32
                    )
                return unused

            lax.fori_loop(0, chunks, accumulate, 0)
            largest_sum = accs[0][0][:, HD:]
            for index, g in tiles[1:]:
                largest_sum = jnp.maximum(largest_sum, accs[index][g][:, HD:])
            bad_ref[0] = jnp.where(jnp.max(largest_sum) <= LIMIT, 0, 1)

        return unused

    lax.fori_loop(0, 2, attempt, 0)
    for tile, (index, g) in enumerate(tiles):
        if last:
            part = accs[0][g]
            result_ref[:, g * HD : (g + 1) * HD] = (part[:, :HD] / part[:, HD:]).astype(
                jnp.bfloat16
            )
        else:
            outs[2 * index + 1][g] = max_ref[tile]


def vertical(name, plan, parts, begin, pieces, micros, last=False):
    groups = len(parts)
    outs = STATE * groups
    scratch = []
    if last:
        outs = (jax.ShapeDtypeStruct((ROWS, COLS), jnp.bfloat16),)
        scratch = [pltpu.VMEM((GROUP, ROWS, 2 * HD), jnp.float32)]
    return pl.pallas_call(
        functools.partial(vertical_kernel, groups, begin, len(pieces), last),
        out_shape=outs,
        in_specs=[smem] + [vmem] * (3 * groups + len(pieces)),
        out_specs=(vmem,) * len(outs),
        scratch_shapes=scratch
        + [
            pltpu.VMEM((CAPACITY, HD), jnp.bfloat16),
            pltpu.VMEM((CAPACITY, 2 * HD), jnp.bfloat16),
            pltpu.VMEM((groups * GROUP, ROWS, HD), jnp.float32),
            pltpu.VMEM((2 if groups == 2 else GROUP, ROWS, CHUNK), jnp.float32),
            pltpu.SMEM((1,), jnp.int32),
        ],
        compiler_params=pltpu.CompilerParams(vmem_limit_bytes=VMEM_LIMIT),
        cost_estimate=cost(micros),
        name=name,
    )(plan, *[q for q, _ in parts], *[x for _, state in parts for x in state],
      *[piece.reshape(32, 2, HALF, HD) for piece in pieces])


def body(queries, keys, values, vert_blocks, slash_offsets):
    core = lax.axis_index("seq") & 1
    keep, send, keep_slot, send_slot = prep(vert_blocks, keys, values)
    recv = swap(send, CORE, 1)
    keep_z = swap(keep_slot, Z, 1)
    recv_z = cross(send_slot)
    mine, theirs = jnp.stack([keep_slot, keep_z]), jnp.stack([recv[:, ROWS:], recv_z])
    one = jnp.where(
        core == 0, jnp.stack([mine, theirs], axis=1), jnp.stack([theirs, mine], axis=1)
    )
    one_z = swap(one, Z, 2)
    plan = make_plan(vert_blocks, one)
    tail = jnp.where(core == 1, keep[:, :ROWS], recv[:, :ROWS])
    tail = tail + one_z[0, 0, :, :1, :1] * 0
    prev = lax.ppermute(tail, "seq", [(i, i + 2) for i in range(126)])
    own, foreign = split(queries, one)
    other = swap(foreign, CORE, 1)
    near_own = band("band_own", False, plan, slash_offsets, own, keep, recv, prev)
    near_other = band("band_other", True, plan, slash_offsets, other, keep, recv, prev)
    two = jnp.concatenate([one, one_z])
    near = []
    for part, axis in ((two[:, :, :, :HALF], Y), (two[:, :, :, HALF:], X)):
        line = jnp.stack([part, swap(part, axis, 1)])
        near.append(jnp.concatenate([line, swap(line, axis, 3)]))
    via_1 = [swap(piece, axis, 1) for piece, axis in zip(near, (X, Y))]
    via_3 = [swap(piece, axis, 3) for piece, axis in zip(near, (X, Y))]
    far = [swap(piece, axis, 1) for piece, axis in zip(via_3, (X, Y))]
    parts = ((own, near_own), (other, near_other))
    state = vertical("near", plan, parts, 0, near, 6)
    parts = ((own, state[:2]), (other, state[2:]))
    pieces = near + via_1 + via_3
    state = vertical("middle", plan, parts, 2, pieces, 12)
    pieces = pieces + far
    (foreign_result,) = vertical("far", plan, ((other, state[2:]),), 6, pieces, 4, True)
    arrived = swap(foreign_result, CORE, 1)
    (result,) = vertical("last", plan, ((own, state[:2]),), 6, pieces, 4, True)
    return jnp.where(
        core == 0,
        jnp.concatenate([result, arrived], axis=1),
        jnp.concatenate([arrived, result], axis=1),
    )


def solution(mesh):
    in_specs = (
        P("seq", "head"),
        P("seq", "head"),
        P("seq", "head"),
        P("head", None),
        P("head", None),
    )
    out_specs = P("seq", "head")
    return jax.shard_map(body, mesh=mesh, in_specs=in_specs, out_specs=out_specs, check_vma=False)
```

```python
import functools

import jax
import jax.numpy as jnp
import numpy as np
from jax import lax
from jax.experimental import pallas as pl
from jax.experimental.pallas import tpu as pltpu
from jax.sharding import PartitionSpec as P

HD = 128
GROUP = 7
BLK = 64
NV = 64
ROWS = 256
HALF = 32
COLS = GROUP * HD
DIMS = (4, 4, 4, 2)
X, Y, Z, CORE = 0, 1, 2, 3
SCALE = HD ** (-0.5) * 1.4426950408889634
LIMIT = 2.0**100
CHUNK = 256
UNROLL = 4
CAPACITY = 2 * NV * HALF + 2 * CHUNK
NT = (((1,), (1,)), ((), ()))
VMEM_LIMIT = 32 * 1024 * 1024

vmem = pl.BlockSpec(memory_space=pltpu.VMEM)
smem = pl.BlockSpec(memory_space=pltpu.SMEM)


def partner_route(axis, mask):
    ids = np.arange(128).reshape(DIMS)
    route = []
    for place in np.ndindex(*DIMS):
        other = list(place)
        other[axis] ^= mask
        route.append((int(ids[place]), int(ids[tuple(other)])))
    return route


def swap(block, axis, mask):
    return lax.ppermute(block, "seq", partner_route(axis, mask))


def cross(block):
    route = [(source, target ^ 1) for source, target in partner_route(Z, 1)]
    return lax.ppermute(block, "seq", route)


def coords():
    device = lax.axis_index("seq")
    return device, device >> 5, (device >> 3) & 3, (device >> 1) & 3, device & 1


def prep_kernel(
    vert_ref, keys_ref, values_ref, keep_ref, send_ref, keep_slot_ref, send_slot_ref
):
    device, _, _, _, core = coords()
    first = device * (ROWS // BLK)

    def find(index, found):
        out = []
        for head in range(2):
            rel = vert_ref[head, index] - first
            inside = (rel >= 0) & (rel < ROWS // BLK)
            out.append(jnp.where(inside, rel, found[head]))
        return tuple(out)

    found = lax.fori_loop(0, NV, find, (jnp.int32(0), jnp.int32(0)), unroll=16)
    for head in range(2):
        cols = slice(head * HD, (head + 1) * HD)
        start = pl.ds(pl.multiple_of(found[head] * BLK, BLK), BLK)

        def fill(out_ref, slot_ref, cols=cols, start=start):
            for which, src in enumerate((keys_ref, values_ref)):
                slot = src[start, cols]
                out_ref[which, :ROWS] = src[:, cols]
                out_ref[which, ROWS:] = slot
                slot_ref[which] = slot

        @pl.when(core == head)
        def _(fill=fill):
            fill(keep_ref, keep_slot_ref)

        @pl.when(core != head)
        def _(fill=fill):
            fill(send_ref, send_slot_ref)


def prep(vert_blocks, keys, values):
    shape = jax.ShapeDtypeStruct((2, ROWS + BLK, HD), jnp.bfloat16)
    slot = jax.ShapeDtypeStruct((2, BLK, HD), jnp.bfloat16)
    return pl.pallas_call(
        prep_kernel,
        out_shape=(shape, shape, slot, slot),
        in_specs=[smem, vmem, vmem],
        out_specs=(vmem, vmem, vmem, vmem),
        name="prep",
    )(vert_blocks, keys, values)


def cost(micros):
    return pl.CostEstimate(flops=int(micros * 1.15e9), bytes_accessed=4 << 20, transcendentals=0)


def plan_kernel(vert_ref, after_ref, plan_ref):
    device, x0, y0, z0, core = coords()
    chip = device >> 1
    base = chip * 8 - 4
    for source in range(8):
        plan_ref[source, 0] = 0
    for slot in range(12):
        plan_ref[8, slot] = 0
    plan_ref[8, 12] = 99
    plan_ref[8, 13] = 99

    def mark(index, unused):
        block = vert_ref[core, index]
        rel = block - base
        owner = block >> 2
        x, y = (owner >> 5) ^ x0, ((owner >> 3) & 3) ^ y0
        x, y = x ^ (x >> 1), y ^ (y >> 1)
        where_in = ((((owner >> 1) & 3) ^ z0) << 1) | (owner & 1)

        @pl.when(block < chip * 8)
        def _():
            for first, outer, inner in ((0, x, y), (1, y, x)):
                source = 2 * outer + first
                number = plan_ref[source, 0]
                plan_ref[source, 1 + number] = (inner << 3) | where_in
                plan_ref[source, 0] = number + 1

        @pl.when((rel >= 0) & (rel < 12))
        def _():
            plan_ref[8, rel] = 1

            @pl.when(rel >= 4)
            def _():
                plan_ref[8, 11 + (rel >> 2)] = rel

        return unused

    lax.fori_loop(0, NV, mark, 0)


def split_kernel(q_ref, after_ref, own_ref, foreign_ref):
    core = coords()[-1]

    @pl.when(core == 0)
    def _():
        own_ref[...] = q_ref[:, :COLS]
        foreign_ref[...] = q_ref[:, COLS:]

    @pl.when(core == 1)
    def _():
        own_ref[...] = q_ref[:, COLS:]
        foreign_ref[...] = q_ref[:, :COLS]


def split(queries, after):
    shape = jax.ShapeDtypeStruct((ROWS, COLS), jnp.bfloat16)
    return pl.pallas_call(
        split_kernel,
        out_shape=(shape, shape),
        in_specs=[vmem, vmem],
        out_specs=(vmem, vmem),
        cost_estimate=cost(1.5),
        name="split",
    )(queries, after)


def make_plan(vert_blocks, after):
    return pl.pallas_call(
        plan_kernel,
        out_shape=jax.ShapeDtypeStruct((9, 128), jnp.int32),
        in_specs=[smem, vmem],
        out_specs=smem,
        cost_estimate=cost(3),
        name="plan",
    )(vert_blocks, after)


def band_kernel(
    foreign, plan_ref, slash_ref, q_ref, keep_ref, recv_ref, prev_ref,
    acc_ref, max_ref, key_ref, value_ref,
):
    device, _, _, _, core = coords()
    base = (device >> 1) * 8 - 4
    middle = slash_ref[core, 0] + slash_ref[core, 1] + slash_ref[core, 2] - 4
    value_ref[:, HD:] = jnp.ones((3 * ROWS, HD), jnp.bfloat16)
    for src, place in ((prev_ref, 0), (keep_ref, 1 + core), (recv_ref, 2 - core)):
        rows = pl.ds(pl.multiple_of(place * ROWS, ROWS), ROWS)
        key_ref[rows, :] = src[0, :ROWS]
        value_ref[rows, :HD] = src[1, :ROWS]
    vert_first, vert_second = plan_ref[8, 12], plan_ref[8, 13]
    row = lax.broadcasted_iota(jnp.int32, (BLK, 6 * BLK), 0)
    col = lax.broadcasted_iota(jnp.int32, (BLK, 6 * BLK), 1)
    piece = col // BLK
    diagonal = (piece == 0) & (col <= row)
    chip_half = 1 - core if foreign else core
    for step in range(4):
        place = chip_half * 4 + (step + 4)
        spots = [place, place - middle, place - 4, vert_first, vert_second]
        on = [None]
        for spot in spots[1:3]:
            on.append((base + spot >= 0) & (plan_ref[8, spot] == 0))
        for spot in spots[3:]:
            on.append(spot < place)
        allowed = diagonal
        for number in range(1, 5):
            allowed = allowed | ((piece == number) & (jnp.where(on[number], 1, 0) == 1))
        safe = [jnp.where(spot < 12, spot, 0) for spot in spots] + [place]
        windows = [pl.ds(pl.multiple_of(spot * BLK, BLK), BLK) for spot in safe]
        keys_here = jnp.concatenate([key_ref[w, :] for w in windows], axis=0)
        values_here = jnp.concatenate([value_ref[w, :] for w in windows], axis=0)
        q_rows = slice(step * BLK, (step + 1) * BLK)
        queries = jnp.concatenate(
            [q_ref[q_rows, g * HD : (g + 1) * HD] for g in range(GROUP)], axis=0
        )
        scores = lax.dot_general(queries, keys_here, NT, preferred_element_type=jnp.float32)
        weights = []
        for g in range(GROUP):
            part = jnp.where(allowed, scores[g * BLK : (g + 1) * BLK] * SCALE, -1e30)
            largest = jnp.max(part, axis=1, keepdims=True)
            weights.append(jnp.exp2(part - largest).astype(jnp.bfloat16))
            max_ref[g, q_rows, :] = jnp.broadcast_to(largest, (BLK, HD))
        mixed = jnp.dot(
            jnp.concatenate(weights, axis=0), values_here, preferred_element_type=jnp.float32
        )
        for g in range(GROUP):
            acc_ref[g, q_rows, :] = mixed[g * BLK : (g + 1) * BLK]


STATE = (
    jax.ShapeDtypeStruct((GROUP, ROWS, 2 * HD), jnp.float32),
    jax.ShapeDtypeStruct((GROUP, ROWS, HD), jnp.float32),
)


def band(name, foreign, plan, slash_offsets, queries, keep, recv, prev):
    return pl.pallas_call(
        functools.partial(band_kernel, foreign),
        out_shape=STATE,
        in_specs=[smem, smem] + [vmem] * 4,
        out_specs=(vmem, vmem),
        scratch_shapes=[
            pltpu.VMEM((3 * ROWS, HD), jnp.bfloat16),
            pltpu.VMEM((3 * ROWS, 2 * HD), jnp.bfloat16),
        ],
        compiler_params=pltpu.CompilerParams(vmem_limit_bytes=VMEM_LIMIT),
        cost_estimate=cost(3),
        name=name,
    )(plan, slash_offsets, queries, keep, recv, prev)


def vertical_kernel(groups, begin, end, last, *refs):
    plan_ref, refs = refs[0], refs[1:]
    queries, refs = refs[:groups], refs[groups:]
    state, refs = refs[: 2 * groups], refs[2 * groups :]
    pieces, outs, scratch = refs[:end], refs[end:-5], refs[-5:]
    key_ref, value_ref, max_ref, score_ref, bad_ref = scratch
    if last:
        result_ref, acc_ref = outs
        accs = [acc_ref]
    else:
        accs = outs[::2]
    tiles = [(index, g) for index in range(groups) for g in range(GROUP)]
    ahead = 2 if len(tiles) % 2 == 0 else len(tiles)
    per_chunk = CHUNK // HALF
    counts = [plan_ref[source, 0] for source in range(end)]
    start = sum(counts[:begin], jnp.int32(0)) // per_chunk * per_chunk
    total = sum(counts, jnp.int32(0))
    stop = total if last else total // per_chunk * per_chunk
    before = jnp.int32(0)
    for source in range(end):

        low = jnp.clip(start - before, 0, counts[source])
        high = jnp.clip(stop - before, 0, counts[source])

        def place(step, unused, source=source, before=before, low=low, high=high):
            for extra in range(UNROLL):
                entry = jnp.minimum(low + step * UNROLL + extra, high - 1)
                code = plan_ref[source, 1 + entry]
                rows = pl.ds(pl.multiple_of((before + entry - start) * HALF, HALF), HALF)
                key_ref[rows, :] = pieces[source][code, 0]
                value_ref[rows, :HD] = pieces[source][code, 1]
                value_ref[rows, HD:] = jnp.ones((HALF, HD), jnp.bfloat16)
            return unused

        lax.fori_loop(0, (high - low + UNROLL - 1) // UNROLL, place, 0)
        before = before + counts[source]
    filled = stop - start
    chunks = (filled + per_chunk - 1) // per_chunk
    if last:

        def pad(step, unused):
            rows = pl.ds(pl.multiple_of(step * HALF, HALF), HALF)
            key_ref[rows, :] = key_ref[:HALF, :]
            value_ref[rows, :] = jnp.zeros((HALF, 2 * HD), jnp.bfloat16)
            return unused

        lax.fori_loop(filled, chunks * per_chunk, pad, 0)

    def scores_of(index, cols, step):
        rows = pl.ds(pl.multiple_of(step * CHUNK, CHUNK), CHUNK)
        return lax.dot_general(
            queries[index][:, cols], key_ref[rows, :], NT, preferred_element_type=jnp.float32
        )

    def tile_scores(tile, step):
        index, g = tiles[tile]
        return scores_of(index, slice(g * HD, (g + 1) * HD), step)

    for tile, (index, g) in enumerate(tiles):
        max_ref[tile] = state[2 * index + 1][g]
    bad_ref[0] = 1

    def attempt(number, unused):
        again = bad_ref[0] == 1

        @pl.when(again & (number == 0))
        def _():
            for index, g in tiles:
                accs[index][g] = state[2 * index][g]

        @pl.when(again & (number == 1))
        def _():
            for index in range(groups):

                def raise_max(step, unused, index=index):
                    g = step % GROUP
                    cols = pl.ds(pl.multiple_of(g * HD, HD), HD)
                    scaled = scores_of(index, cols, step // GROUP) * SCALE
                    top = jnp.max(scaled, axis=1, keepdims=True)
                    max_ref[index * GROUP + g] = jnp.maximum(max_ref[index * GROUP + g], top)
                    return unused

                def rescale(g, unused, index=index):
                    factor = jnp.exp2(state[2 * index + 1][g] - max_ref[index * GROUP + g])
                    accs[index][g] = state[2 * index][g] * jnp.concatenate([factor] * 2, axis=1)
                    return unused

                lax.fori_loop(0, chunks * GROUP, raise_max, 0)
                lax.fori_loop(0, GROUP, rescale, 0)

        @pl.when(again)
        def _():
            for tile in range(ahead):
                score_ref[tile] = tile_scores(tile, 0)

            def accumulate(step, unused):
                rows = pl.ds(pl.multiple_of(step * CHUNK, CHUNK), CHUNK)
                for tile, (index, g) in enumerate(tiles):
                    later = tile + ahead
                    coming = tile_scores(later % len(tiles), step + later // len(tiles))
                    largest = jnp.concatenate([max_ref[tile]] * (CHUNK // HD), axis=1)
                    shifted = score_ref[tile % ahead] * SCALE - largest
                    score_ref[tile % ahead] = coming
                    weights = jnp.exp2(shifted).astype(jnp.bfloat16)
                    accs[index][g] += jnp.dot(
                        weights, value_ref[rows, :], preferred_element_type=jnp.float32
                    )
                return unused

            lax.fori_loop(0, chunks, accumulate, 0)
            largest_sum = accs[0][0][:, HD:]
            for index, g in tiles[1:]:
                largest_sum = jnp.maximum(largest_sum, accs[index][g][:, HD:])
            bad_ref[0] = jnp.where(jnp.max(largest_sum) <= LIMIT, 0, 1)

        return unused

    lax.fori_loop(0, 2, attempt, 0)
    for tile, (index, g) in enumerate(tiles):
        if last:
            part = accs[0][g]
            result_ref[:, g * HD : (g + 1) * HD] = (part[:, :HD] / part[:, HD:]).astype(
                jnp.bfloat16
            )
        else:
            outs[2 * index + 1][g] = max_ref[tile]


def vertical(name, plan, parts, begin, pieces, micros, last=False):
    groups = len(parts)
    outs = STATE * groups
    scratch = []
    if last:
        outs = (jax.ShapeDtypeStruct((ROWS, COLS), jnp.bfloat16),)
        scratch = [pltpu.VMEM((GROUP, ROWS, 2 * HD), jnp.float32)]
    return pl.pallas_call(
        functools.partial(vertical_kernel, groups, begin, len(pieces), last),
        out_shape=outs,
        in_specs=[smem] + [vmem] * (3 * groups + len(pieces)),
        out_specs=(vmem,) * len(outs),
        scratch_shapes=scratch
        + [
            pltpu.VMEM((CAPACITY, HD), jnp.bfloat16),
            pltpu.VMEM((CAPACITY, 2 * HD), jnp.bfloat16),
            pltpu.VMEM((groups * GROUP, ROWS, HD), jnp.float32),
            pltpu.VMEM((2 if groups == 2 else GROUP, ROWS, CHUNK), jnp.float32),
            pltpu.SMEM((1,), jnp.int32),
        ],
        compiler_params=pltpu.CompilerParams(vmem_limit_bytes=VMEM_LIMIT),
        cost_estimate=cost(micros),
        name=name,
    )(plan, *[q for q, _ in parts], *[x for _, state in parts for x in state],
      *[piece.reshape(32, 2, HALF, HD) for piece in pieces])


def body(queries, keys, values, vert_blocks, slash_offsets):
    core = lax.axis_index("seq") & 1
    keep, send, keep_slot, send_slot = prep(vert_blocks, keys, values)
    recv = swap(send, CORE, 1)
    keep_z = swap(keep_slot, Z, 1)
    recv_z = cross(send_slot)
    mine, theirs = jnp.stack([keep_slot, keep_z]), jnp.stack([recv[:, ROWS:], recv_z])
    one = jnp.where(
        core == 0, jnp.stack([mine, theirs], axis=1), jnp.stack([theirs, mine], axis=1)
    )
    one_z = swap(one, Z, 2)
    joined = one[0, 0, 0, :16]
    plan = make_plan(vert_blocks, joined)
    tail = jnp.where(core == 1, keep[:, :ROWS], recv[:, :ROWS])
    tail = tail + one_z[0, 0, :, :1, :1] * 0
    prev = lax.ppermute(tail, "seq", [(i, i + 2) for i in range(126)])
    own, foreign = split(queries, joined)
    other = swap(foreign, CORE, 1)
    near_own = band("band_own", False, plan, slash_offsets, own, keep, recv, prev)
    near_other = band("band_other", True, plan, slash_offsets, other, keep, recv, prev)
    two = jnp.concatenate([one, one_z])
    near = []
    for part, axis in ((two[:, :, :, :HALF], Y), (two[:, :, :, HALF:], X)):
        line = jnp.stack([part, swap(part, axis, 1)])
        near.append(jnp.concatenate([line, swap(line, axis, 3)]))
    via_1 = [swap(piece, axis, 1) for piece, axis in zip(near, (X, Y))]
    via_3 = [swap(piece, axis, 3) for piece, axis in zip(near, (X, Y))]
    far = [swap(piece, axis, 1) for piece, axis in zip(via_3, (X, Y))]
    parts = ((own, near_own), (other, near_other))
    state = vertical("near", plan, parts, 0, near, 6)
    parts = ((own, state[:2]), (other, state[2:]))
    pieces = near + via_1 + via_3
    state = vertical("middle", plan, parts, 2, pieces, 12)
    pieces = pieces + far
    (foreign_result,) = vertical("far", plan, ((other, state[2:]),), 6, pieces, 4, True)
    arrived = swap(foreign_result, CORE, 1)
    (result,) = vertical("last", plan, ((own, state[:2]),), 6, pieces, 4, True)
    return jnp.where(
        core == 0,
        jnp.concatenate([result, arrived], axis=1),
        jnp.concatenate([arrived, result], axis=1),
    )


def solution(mesh):
    in_specs = (
        P("seq", "head"),
        P("seq", "head"),
        P("seq", "head"),
        P("head", None),
        P("head", None),
    )
    out_specs = P("seq", "head")
    return jax.shard_map(body, mesh=mesh, in_specs=in_specs, out_specs=out_specs, check_vma=False)
```
